256 devices in a mesh: dp: 8 (over z), tensor: 32 (over x, y, core).
Axes of the slice: x: 4, y: 4, z: 8, core: 2. Of those that a mesh axis runs over, the one named last changes fastest.
Arguments:
- tokens: bfloat16 [4096, 2304], P(('dp', 'tensor')), may hold values from -6 to 6
- cotangent: bfloat16 [4096, 2304], P(('dp', 'tensor')), may hold values from -20 to 20
- gate_weight: bfloat16 [2304, 18432], P(None, 'tensor'), may hold values from -0.125 to 0.125
- up_weight: bfloat16 [2304, 18432], P(None, 'tensor'), may hold values from -0.1875 to 0.1875
- down_weight: bfloat16 [18432, 2304], P('tensor'), may hold values from -0.046875 to 0.046875
Outputs:
- input_grad: bfloat16 [4096, 2304], P(('dp', 'tensor'))
- grad_gate: float32 [2304, 18432], P('dp', 'tensor')
- grad_up: float32 [2304, 18432], P('dp', 'tensor')
- grad_down: float32 [18432, 2304], P('tensor', 'dp')
The draws below stay inside these ranges and needn't reach their ends.
All inputs are finite; a program needn't handle non-finite values.
Results may differ from the reference program's by a relative error of at most 0.017.
Values may be sent and summed in bfloat16 or wider, within the bound.
No kernel may reach another device: no remote copies, remote signals or barrier semaphores. Data moves between devices by JAX's collectives and lax.ppermute only.
A program may use at most 128 MiB of HBM per device.

```python
import math
import jax
import jax.numpy as jnp
from jax import lax

D = 2304
FF = 18432
SEQ = 256
TOKENS = 4096


def draw_tokens(key, part):
    key = jax.random.fold_in(key, 13)
    entry_key = jax.random.fold_in(key, 0)
    base = jnp.clip(jax.random.normal(entry_key, (TOKENS, D), jnp.float32), -6.0, 6.0)
    return base.astype(jnp.bfloat16)


def draw_cotangent(key, part):
    key = jax.random.fold_in(key, 11)
    level_key, entry_key = jax.random.split(key)
    levels = jnp.exp(jax.random.uniform(level_key, (TOKENS // SEQ,), jnp.float32, jnp.log(0.25), jnp.log(4.0)))
    base = jnp.clip(jax.random.normal(entry_key, (TOKENS, D), jnp.float32), -5.0, 5.0)
    row_levels = jnp.repeat(levels, SEQ)
    return (base * row_levels[:, None]).astype(jnp.bfloat16)


def draw_up_weight(key, part):
    key = jax.random.fold_in(key, 12)
    ramp = 0.6 * 3.0 ** (jnp.arange(FF, dtype=jnp.float32) / FF)
    base = jnp.clip(jax.random.normal(key, (D, FF), jnp.float32), -5.0, 5.0)
    return (base * ramp[None, :] / jnp.sqrt(jnp.float32(D))).astype(jnp.bfloat16)


def block_scale(own_key, shape, cuts, low, largest):
    level, own = 1.0, jax.random.fold_in(own_key, 6)
    for axis_at, blocks in cuts:
        steps = jnp.exp(jax.random.uniform(jax.random.fold_in(own, axis_at), (blocks,), jnp.float32, low / len(cuts), largest / len(cuts)))
        level = level * jnp.repeat(steps, shape[axis_at] // blocks).reshape([-1 if axis == axis_at else 1 for axis in range(len(shape))])
    return level


def bell_draw(own_key, extent, width, bound, shards=(), kind=jnp.bfloat16):
    result = width * jax.random.normal(own_key, extent, jnp.float32)
    if shards:
        result = result * block_scale(own_key, extent, shards, -0.22, 0.18)
    return jnp.clip(result, -bound, bound).astype(kind)


def setup_inputs(seed: int = 0) -> dict:
    arg_keys = jax.random.split(jax.random.key(seed), 6)
    return {
        "tokens": draw_tokens(jax.random.fold_in(arg_keys[5], 71), 0),
        "cotangent": draw_cotangent(jax.random.fold_in(arg_keys[5], 71), 0),
        "gate_weight": bell_draw(arg_keys[2], (D, FF), D ** -0.5, 0.125, ((1, 32),)),
        "up_weight": draw_up_weight(jax.random.fold_in(arg_keys[5], 71), 0),
        "down_weight": bell_draw(arg_keys[4], (FF, D), FF ** -0.5, 0.046875, ((0, 32),)),
    }


GELU_ROOT = math.sqrt(2.0 / math.pi)
GELU_CUBIC = 0.044715

def gelu_pair(value):
    inner = GELU_ROOT * (value + GELU_CUBIC * value * value * value)
    tangent = jnp.tanh(inner)
    activ = 0.5 * value * (1.0 + tangent)
    slope = 0.5 * (1.0 + tangent) + 0.5 * value * (1.0 - tangent * tangent) * GELU_ROOT * (1.0 + 3.0 * GELU_CUBIC * value * value)
    return (activ, slope)

def reference(tokens, cotangent, gate_weight, up_weight, down_weight):
    pre_gate = jnp.dot(tokens, gate_weight, preferred_element_type=jnp.float32)
    pre_up = jnp.dot(tokens, up_weight, preferred_element_type=jnp.float32)
    activ, slope = gelu_pair(pre_gate)
    hidden = (activ * pre_up).astype(jnp.bfloat16)
    grad_hidden = jnp.dot(cotangent, down_weight.T, preferred_element_type=jnp.float32)
    grad_pre_gate = (grad_hidden * pre_up * slope).astype(jnp.bfloat16)
    grad_pre_up = (grad_hidden * activ).astype(jnp.bfloat16)
    input_grad = (jnp.dot(grad_pre_gate, gate_weight.T, preferred_element_type=jnp.float32) + jnp.dot(grad_pre_up, up_weight.T, preferred_element_type=jnp.float32)).astype(jnp.bfloat16)
    total = TOKENS // SEQ
    inputs_ex = tokens.reshape(total, SEQ, D).astype(jnp.float32)
    cotan_ex = cotangent.reshape(total, SEQ, D).astype(jnp.float32)
    gate_ex = grad_pre_gate.reshape(total, SEQ, FF).astype(jnp.float32)
    up_ex = grad_pre_up.reshape(total, SEQ, FF).astype(jnp.float32)
    hidden_ex = hidden.reshape(total, SEQ, FF).astype(jnp.float32)
    gram_in = jnp.einsum('esd,etd->est', inputs_ex, inputs_ex)
    gram_cot = jnp.einsum('esd,etd->est', cotan_ex, cotan_ex)
    gram_gate = jnp.einsum('esf,etf->est', gate_ex, gate_ex)
    gram_up = jnp.einsum('esf,etf->est', up_ex, up_ex)
    gram_hid = jnp.einsum('esf,etf->est', hidden_ex, hidden_ex)
    norm_sq = lax.optimization_barrier(jnp.sum(gram_in * (gram_gate + gram_up) + gram_hid * gram_cot, axis=(1, 2)))
    clip_level = math.sqrt(SEQ * D * (FF // 2 + D))
    factor = math.sqrt(D * FF) / jnp.maximum(clip_level, jnp.sqrt(norm_sq))

    def accumulate(carry, pieces):
        inputs_one, cotan_one, gate_one, up_one, hidden_one, scale = pieces
        new_gate = carry[0] + scale * jnp.dot(inputs_one.T, gate_one, preferred_element_type=jnp.float32)
        new_up = carry[1] + scale * jnp.dot(inputs_one.T, up_one, preferred_element_type=jnp.float32)
        new_down = carry[2] + scale * jnp.dot(hidden_one.T, cotan_one, preferred_element_type=jnp.float32)
        return ((new_gate, new_up, new_down), None)
    start_sums = (jnp.zeros((D, FF), jnp.float32), jnp.zeros((D, FF), jnp.float32), jnp.zeros((FF, D), jnp.float32))
    pieces = (tokens.reshape(total, SEQ, D), cotangent.reshape(total, SEQ, D), grad_pre_gate.reshape(total, SEQ, FF), grad_pre_up.reshape(total, SEQ, FF), hidden.reshape(total, SEQ, FF), factor)
    sums, unused = lax.scan(accumulate, start_sums, pieces)
    return (input_grad, sums[0], sums[1], sums[2])
```

```python
import math

import jax
import jax.numpy as jnp
import numpy as np
from jax import lax
from jax.experimental import pallas as pl
from jax.experimental.pallas import tpu as pltpu
from jax.sharding import PartitionSpec as P

D = 2304
FF = 18432
SEQ = 256
NX = 4
NY = 4
NZ = 8
CHUNK = D // NZ
PARTS = 4
HALF = CHUNK // 2
SUB = CHUNK // PARTS
DEVICES = 2 * NX * NY
TILE = 256
GELU_ROOT = math.sqrt(2.0 / math.pi)
GELU_CUBIC = 0.044715
BF = jnp.bfloat16
F32 = jnp.float32


def flat(x, y, c):
    return ((x % NX) * NY + (y % NY)) * 2 + c


def device_perm(move):
    return [
        (flat(x, y, c), flat(*move(x, y, c)))
        for x in range(NX)
        for y in range(NY)
        for c in range(2)
    ]


def y_perm(k):
    return device_perm(lambda x, y, c: (x, y + k, c))


def x_perm(k):
    return device_perm(lambda x, y, c: (x + k, y, c))


def round_perm(k):
    return device_perm(lambda x, y, c: (x + k + 2 * c, y, x // 2))


def inverse(perm):
    return [(b, a) for a, b in perm]


SWAP = device_perm(lambda x, y, c: (x, y, 1 - c))


def send(value, perm):
    return lax.ppermute(value, "tensor", perm)


def gelu_pair(value):
    inner = GELU_ROOT * (value + GELU_CUBIC * value * value * value)
    tangent = jnp.tanh(inner)
    activ = 0.5 * value * (1.0 + tangent)
    slope = 0.5 * (1.0 + tangent) + 0.5 * value * (1.0 - tangent * tangent) * GELU_ROOT * (
        1.0 + 3.0 * GELU_CUBIC * value * value
    )
    return (activ, slope)


def gather_tokens(shard):
    column = jnp.concatenate([shard] + [send(shard, y_perm(k)) for k in (1, 2, 3)], 0)
    rounds = [send(column, round_perm(k)).reshape(4, 16, D) for k in range(4)]
    return jnp.stack(rounds, 1).reshape(SEQ, D)


def gather_cotangent(shard):
    row = jnp.concatenate([send(shard, round_perm(k)) for k in range(4)], 0)
    return jnp.concatenate([row] + [send(row, y_perm(k)) for k in (1, 2, 3)], 0)


def after(value, *others):
    return lax.optimization_barrier((value, *others))[0]


def dot_nt(a, b):
    return lax.dot_general(a, b, (((1,), (1,)), ((), ())), preferred_element_type=F32)


def dot_tn(a, b):
    return lax.dot_general(a, b, (((0,), (0,)), ((), ())), preferred_element_type=F32)


def example(tok, cot, gate_t, up_t, down):
    pre_gate = dot_nt(gate_t, tok)
    pre_up = dot_nt(up_t, tok)
    activ, slope = gelu_pair(pre_gate)
    hidden = (activ * pre_up).astype(BF)
    grad_hidden = dot_nt(down, cot)
    grad_gate = (grad_hidden * pre_up * slope).astype(BF)
    grad_up = (grad_hidden * activ).astype(BF)
    norm = jnp.sum(
        dot_nt(tok, tok) * (dot_tn(grad_gate, grad_gate) + dot_tn(grad_up, grad_up))
        + dot_nt(cot, cot) * dot_tn(hidden, hidden),
        axis=0,
    )
    return hidden, grad_gate, grad_up, norm


def in_vmem(value):
    return pltpu.with_memory_space_constraint(value, pltpu.VMEM)


def turn_kernel(first, second, out):
    @pl.loop(0, D // 128)
    def _(i):
        at = pl.ds(pl.multiple_of(i * 128, 128), 128)
        out[at, :SEQ] = first[:, at].T
        out[at, SEQ:] = second[:, at].T


def turn(first, second):
    vmem = pl.BlockSpec(memory_space=pltpu.VMEM)
    return pl.pallas_call(
        turn_kernel,
        in_specs=[vmem, vmem],
        out_specs=vmem,
        out_shape=pltpu.VMEM((D, 2 * SEQ), BF),
        compiler_params=pltpu.CompilerParams(vmem_limit_bytes=12 * 2**20),
        cost_estimate=pl.CostEstimate(flops=4 * SEQ * D, bytes_accessed=8 * SEQ * D, transcendentals=0),
    )(in_vmem(first), in_vmem(second))


CLIP = math.sqrt(SEQ * D * (FF // 2 + D))
REACH = math.sqrt(D * FF)


def outer_kernel(
    where, norms, tok, cot, gg_a, gu_a, hid_a, gg_b, gu_b, hid_b, out, both, third, ready, sems,
):
    factor = REACH / jnp.maximum(CLIP, jnp.sqrt(jnp.sum(norms[...], axis=1, keepdims=True)))
    mine = jnp.where(where[1] == 0, factor[:1], factor[1:])
    theirs = jnp.where(where[1] == 0, factor[1:], factor[:1])
    width = third.shape[1]
    for at, scale, (gg, gu, hid) in (
        (slice(0, SEQ), mine, (gg_a, gu_a, hid_a)),
        (slice(SEQ, 2 * SEQ), theirs, (gg_b, gu_b, hid_b)),
    ):
        joined = jnp.concatenate([gg[...], gu[...]], 0).astype(F32) * scale
        both[at, :] = joined.astype(BF).T
        third[at, :] = (hid[...].astype(F32) * scale).astype(BF).T

    def push(slot, i):
        block = lax.rem(i + NZ - where[0], NZ)
        return pltpu.make_async_copy(ready.at[slot], out.at[block], sems.at[slot])

    @pl.loop(0, NZ)
    def _(i):
        slot = lax.rem(i, 2)

        @pl.when(i >= 2)
        def _():
            push(slot, i - 2).wait()

        at = pl.ds(pl.multiple_of(i * CHUNK, CHUNK), CHUNK)
        ready[slot, :, : 2 * width] = jnp.dot(tok[at, :], both[...], preferred_element_type=F32).astype(BF)
        ready[slot, :, 2 * width :] = jnp.dot(cot[at, :], third[...], preferred_element_type=F32).astype(BF)
        push(slot, i).start()

    push(0, NZ - 2).wait()
    push(1, NZ - 1).wait()


def outer_products(where, norms, tok, cot, grads):
    width = grads[0].shape[0]
    vmem = pl.BlockSpec(memory_space=pltpu.VMEM)
    smem = pl.BlockSpec(memory_space=pltpu.SMEM)
    return pl.pallas_call(
        outer_kernel,
        in_specs=[smem] + [vmem] * 9,
        out_specs=pl.BlockSpec(memory_space=pltpu.HBM),
        scratch_shapes=[
            pltpu.VMEM((2 * SEQ, 2 * width), BF),
            pltpu.VMEM((2 * SEQ, width), BF),
            pltpu.VMEM((2, CHUNK, 3 * width), BF),
            pltpu.SemaphoreType.DMA((2,)),
        ],
        out_shape=pltpu.HBM((NZ, CHUNK, 3 * width), BF),
        compiler_params=pltpu.CompilerParams(vmem_limit_bytes=16 * 2**20),
        cost_estimate=pl.CostEstimate(
            flops=12 * SEQ * D * width,
            bytes_accessed=8 * SEQ * D + 6 * D * width + 12 * SEQ * width,
            transcendentals=0,
        ),
    )(where, *map(in_vmem, (norms, tok, cot, *grads)))


def backward_kernel(slots, gg_a, gu_a, gg_b, gu_b, gate, up, out, both_a, both_b):
    @pl.when(pl.program_id(0) == 0)
    def _():
        both_a[...] = jnp.concatenate([gg_a[...], gu_a[...]], 0).T
        both_b[...] = jnp.concatenate([gg_b[...], gu_b[...]], 0).T

    width = gate.shape[0]
    for at, both in ((0, both_a), (1, both_b)):
        value = jnp.dot(both[:, :width], gate[...], preferred_element_type=F32)
        value = value + jnp.dot(both[:, width:], up[...], preferred_element_type=F32)
        value = value.astype(BF).reshape(SEQ // 16, 16, TILE)
        for i in range(SEQ // 16):
            out[slots[at * (SEQ // 16) + i]] = value[i]


def backward(slots, grads, gate_t, up_t):
    width = gate_t.shape[0]
    part = pl.BlockSpec((width, TILE), lambda i, slots: (0, i))
    whole = pl.BlockSpec((width, SEQ), lambda i, slots: (0, 0))
    return pl.pallas_call(
        backward_kernel,
        grid_spec=pltpu.PrefetchScalarGridSpec(
            num_scalar_prefetch=1,
            grid=(D // TILE,),
            in_specs=[whole] * 4 + [part] * 2,
            out_specs=pl.BlockSpec((DEVICES, 16, TILE), lambda i, slots: (0, 0, i)),
            scratch_shapes=[pltpu.VMEM((SEQ, 2 * width), BF)] * 2,
        ),
        out_shape=pltpu.HBM((DEVICES, 16, D), BF),
        compiler_params=pltpu.CompilerParams(vmem_limit_bytes=14 * 2**20),
        cost_estimate=pl.CostEstimate(
            flops=8 * SEQ * D * width,
            bytes_accessed=4 * D * width + 4 * SEQ * D + 8 * SEQ * width,
            transcendentals=0,
        ),
    )(slots, *grads, gate_t, up_t)


def owners():
    table = np.zeros((DEVICES, DEVICES), np.int32)
    for place in range(DEVICES):
        x, y, core = place // (2 * NY), (place // 2) % NY, place % 2
        for at, example in enumerate((core, 1 - core)):
            for j in range(NY):
                for k in range(4):
                    near = (x - k) % NX
                    here = near // 2 == example
                    table[place, 16 * at + 4 * j + k] = flat(near if here else near + 2, y - j, 0 if here else 1)
    return table


def all_sum(value):
    for perms in ([SWAP], [x_perm(k) for k in (1, 2, 3)], [y_perm(k) for k in (1, 2, 3)]):
        value = value + sum(send(value, p) for p in perms)
    return value


def exchange(value):
    return lax.all_to_all(value, "tensor", split_axis=0, concat_axis=0, tiled=True)


def body(tokens, cotangent, gate_weight, up_weight, down):
    place = lax.axis_index("tensor")
    where = jnp.stack([lax.axis_index("dp"), place % 2]).astype(jnp.int32)
    slots = lax.dynamic_index_in_dim(jnp.asarray(owners()), place, 0, False)
    order = jnp.where((jnp.arange(2) + place) % 2 == 0, 1.0, 0.0).astype(F32)[:, None]
    order = jnp.broadcast_to(order, (2, SEQ))
    tokens, cotangent, where, slots, order = lax.optimization_barrier(
        (tokens, cotangent, where, slots, order)
    )
    gate_t, up_t = gate_weight.T, up_weight.T
    tok_a = gather_tokens(tokens)
    cot_a = gather_cotangent(cotangent)
    tok_b = send(tok_a, SWAP)
    cot_b = send(cot_a, SWAP)
    hid_a, gg_a, gu_a, norm_a = example(tok_a, cot_a, gate_t, up_t, down)
    hid_b, gg_b, gu_b, norm_b = example(tok_b, cot_b, gate_t, up_t, down)
    pair = order * norm_a[None] + (1.0 - order) * norm_b[None]
    norms = all_sum(pair)

    late, cot_a, cot_b = lax.optimization_barrier(((gg_a, gu_a, gg_b, gu_b), cot_a, cot_b, pair))[:3]
    partial = backward(slots, late, gate_t, up_t)
    turned_cot = turn(cot_a, cot_b)
    turned_tok = turn(tok_a, tok_b)
    norms, partial, turned_cot = lax.optimization_barrier((norms, partial, turned_cot))
    grads = (gg_a, gu_a, hid_a, gg_b, gu_b, hid_b)
    products = outer_products(where, norms, turned_tok, turned_cot, grads)
    partial = after(partial, products)
    returned = exchange(partial.reshape(DEVICES * 16, D))

    def local(k, part):
        return products[k % NZ, part * SUB : (part + 1) * SUB]

    rings = {s: [(i, (i + s) % NZ) for i in range(NZ)] for s in (1, -1)}
    lanes = [(0, 1), (2, -1), (1, 1), (3, -1)]
    held = {p: local(-s, p) for p, s in lanes}
    last = held[3]
    for step in range(NZ - 1):
        for p, s in lanes:
            value = lax.ppermute(held[p], "dp", rings[s])
            value, last = lax.optimization_barrier((value, last))
            value = value.astype(F32) + local(-s * (step + 2), p).astype(F32)
            held[p] = last = value.astype(BF) if step < NZ - 2 else value
        if step == 5:
            returned = after(returned, last)
            input_grad = jnp.sum(returned.reshape(DEVICES, 16, D).astype(F32), 0).astype(BF)
    totals = jnp.concatenate([held[p] for p in range(PARTS)], 0)
    width = gate_t.shape[0]
    return (
        input_grad,
        totals[:, :width],
        totals[:, width : 2 * width],
        totals[:, 2 * width :].T,
    )


def solution(mesh):
    rows = P(("dp", "tensor"), None)
    return jax.shard_map(
        body,
        mesh=mesh,
        in_specs=(rows, rows, P(None, "tensor"), P(None, "tensor"), P("tensor", None)),
        out_specs=(rows, P("dp", "tensor"), P("dp", "tensor"), P("tensor", "dp")),
        check_vma=False,
    )
```

```python
import functools
import math

import jax
import jax.numpy as jnp
import numpy as np
from jax import lax
from jax.experimental import pallas as pl
from jax.experimental.pallas import tpu as pltpu
from jax.sharding import PartitionSpec as P

D = 2304
FF = 18432
SEQ = 256
NX = 4
NY = 4
NZ = 8
CHUNK = D // NZ
PARTS = 4
HALF = CHUNK // 2
SUB = CHUNK // PARTS
DEVICES = 2 * NX * NY
TILE = 256
GELU_ROOT = math.sqrt(2.0 / math.pi)
GELU_CUBIC = 0.044715
BF = jnp.bfloat16
F32 = jnp.float32


def flat(x, y, c):
    return ((x % NX) * NY + (y % NY)) * 2 + c


def device_perm(move):
    return [
        (flat(x, y, c), flat(*move(x, y, c)))
        for x in range(NX)
        for y in range(NY)
        for c in range(2)
    ]


def y_perm(k):
    return device_perm(lambda x, y, c: (x, y + k, c))


def x_perm(k):
    return device_perm(lambda x, y, c: (x + k, y, c))


def round_perm(k):
    return device_perm(lambda x, y, c: (x + k + 2 * c, y, x // 2))


def inverse(perm):
    return [(b, a) for a, b in perm]


SWAP = device_perm(lambda x, y, c: (x, y, 1 - c))


def send(value, perm):
    return lax.ppermute(value, "tensor", perm)


def gelu_pair(value):
    inner = GELU_ROOT * (value + GELU_CUBIC * value * value * value)
    tangent = jnp.tanh(inner)
    activ = 0.5 * value * (1.0 + tangent)
    slope = 0.5 * (1.0 + tangent) + 0.5 * value * (1.0 - tangent * tangent) * GELU_ROOT * (
        1.0 + 3.0 * GELU_CUBIC * value * value
    )
    return (activ, slope)


def gather(tokens, cotangent):
    shard = jnp.concatenate([tokens, cotangent], 0)
    column = [shard] + [send(shard, y_perm(k)) for k in (1, 2, 3)]
    column = jnp.concatenate([v[:16] for v in column] + [v[16:] for v in column], 0)
    rounds = [send(column, round_perm(k)) for k in range(4)]
    return jnp.concatenate([v[:64] for v in rounds], 0), jnp.concatenate([v[64:] for v in rounds], 0)


def after(value, *others):
    return lax.optimization_barrier((value, *others))[0]


def dot_nt(a, b):
    return lax.dot_general(a, b, (((1,), (1,)), ((), ())), preferred_element_type=F32)


def dot_tn(a, b):
    return lax.dot_general(a, b, (((0,), (0,)), ((), ())), preferred_element_type=F32)


def example(tok, cot, gate_t, up_t, down):
    pre_gate = dot_nt(gate_t, tok)
    pre_up = dot_nt(up_t, tok)
    activ, slope = gelu_pair(pre_gate)
    hidden = (activ * pre_up).astype(BF)
    grad_hidden = dot_nt(down, cot)
    grad_gate = (grad_hidden * pre_up * slope).astype(BF)
    grad_up = (grad_hidden * activ).astype(BF)
    norm = jnp.sum(
        dot_nt(tok, tok) * (dot_tn(grad_gate, grad_gate) + dot_tn(grad_up, grad_up))
        + dot_nt(cot, cot) * dot_tn(hidden, hidden),
        axis=0,
    )
    return hidden, grad_gate, grad_up, norm


def in_vmem(value):
    return pltpu.with_memory_space_constraint(value, pltpu.VMEM)


def turn_kernel(first, second, out):
    @pl.loop(0, D // 128)
    def _(i):
        at = pl.ds(pl.multiple_of(i * 128, 128), 128)
        out[at, :SEQ] = first[:, at].T
        out[at, SEQ:] = second[:, at].T


def turn(first, second):
    vmem = pl.BlockSpec(memory_space=pltpu.VMEM)
    return pl.pallas_call(
        turn_kernel,
        in_specs=[vmem, vmem],
        out_specs=vmem,
        out_shape=pltpu.VMEM((D, 2 * SEQ), BF),
        compiler_params=pltpu.CompilerParams(vmem_limit_bytes=12 * 2**20),
        cost_estimate=pl.CostEstimate(flops=4 * SEQ * D, bytes_accessed=8 * SEQ * D, transcendentals=0),
    )(in_vmem(first), in_vmem(second))


CLIP = math.sqrt(SEQ * D * (FF // 2 + D))
REACH = math.sqrt(D * FF)


def first_kernel(
    where, norms, tok, cot, gg_a, gu_a, hid_a, gg_b, gu_b, hid_b, up_0, up_1, down_0, down_1, both, third,
):
    factor = REACH / jnp.maximum(CLIP, jnp.sqrt(jnp.sum(norms[...], axis=1, keepdims=True)))
    mine = jnp.where(where[1] == 0, factor[:1], factor[1:])
    theirs = jnp.where(where[1] == 0, factor[1:], factor[:1])
    width = third.shape[1]
    for at, scale, (gg, gu, hid) in (
        (slice(0, SEQ), mine, (gg_a, gu_a, hid_a)),
        (slice(SEQ, 2 * SEQ), theirs, (gg_b, gu_b, hid_b)),
    ):
        joined = jnp.concatenate([gg[...], gu[...]], 0).astype(F32) * scale
        both[at, :] = joined.astype(BF).T
        third[at, :] = (hid[...].astype(F32) * scale).astype(BF).T

    fill_parts(where, tok, cot, both, third, (up_0, up_1, down_0, down_1), 1)


def fill_parts(where, tok, cot, both, third, parts, distance):
    width = third.shape[1]
    for hop, start, targets in ((NZ - distance, 0, parts[:2]), (distance, HALF, parts[2:])):
        chunk = lax.rem(where[0] + hop, NZ)
        at = pl.ds(pl.multiple_of(chunk * CHUNK + start, 16), HALF)
        left = jnp.dot(tok[at, :], both[...], preferred_element_type=F32)
        right = jnp.dot(cot[at, :], third[...], preferred_element_type=F32)
        for i, target in enumerate(targets):
            rows = slice(i * SUB, (i + 1) * SUB)
            target[:, : 2 * width] = left[rows].astype(BF)
            target[:, 2 * width :] = right[rows].astype(BF)


def first_products(where, norms, tok, cot, grads):
    width = grads[0].shape[0]
    vmem = pl.BlockSpec(memory_space=pltpu.VMEM)
    smem = pl.BlockSpec(memory_space=pltpu.SMEM)
    *firsts, both, third = pl.pallas_call(
        first_kernel,
        in_specs=[smem] + [vmem] * 9,
        out_specs=[vmem] * (PARTS + 2),
        out_shape=[pltpu.VMEM((SUB, 3 * width), BF)] * PARTS
        + [pltpu.VMEM((2 * SEQ, n * width), BF) for n in (2, 1)],
        compiler_params=pltpu.CompilerParams(vmem_limit_bytes=12 * 2**20),
        cost_estimate=pl.CostEstimate(
            flops=12 * SEQ * HALF * width, bytes_accessed=12 * SEQ * width, transcendentals=0
        ),
    )(where, *map(in_vmem, (norms, tok, cot, *grads)))
    return firsts, both, third


def second_kernel(where, tok, cot, both, third, up_0, up_1, down_0, down_1):
    fill_parts(where, tok, cot, both, third, (up_0, up_1, down_0, down_1), 2)


def second_products(where, tok, cot, both, third):
    width = third.shape[1]
    vmem = pl.BlockSpec(memory_space=pltpu.VMEM)
    smem = pl.BlockSpec(memory_space=pltpu.SMEM)
    return pl.pallas_call(
        second_kernel,
        in_specs=[smem] + [vmem] * 4,
        out_specs=[vmem] * PARTS,
        out_shape=[pltpu.VMEM((SUB, 3 * width), BF)] * PARTS,
        compiler_params=pltpu.CompilerParams(vmem_limit_bytes=8 * 2**20),
        cost_estimate=pl.CostEstimate(
            flops=12 * SEQ * HALF * width, bytes_accessed=12 * SEQ * width, transcendentals=0
        ),
    )(where, *map(in_vmem, (tok, cot, both, third)))


def rest_kernel(hops, where, tok, cot, both, third, out, *scratch):
    width = third.shape[1]
    copies = []
    for i, hop in enumerate(hops):
        target = out.at[i]
        if scratch:
            ready, sems = scratch
            if i >= 2:
                copies[i - 2].wait()
            target = ready.at[i % 2]
        chunk = lax.rem(where[0] + hop, NZ)
        at = pl.ds(pl.multiple_of(chunk * CHUNK, CHUNK), CHUNK)
        target[:, : 2 * width] = jnp.dot(tok[at, :], both[...], preferred_element_type=F32).astype(BF)
        target[:, 2 * width :] = jnp.dot(cot[at, :], third[...], preferred_element_type=F32).astype(BF)
        if scratch:
            copies.append(pltpu.make_async_copy(target, out.at[i], sems.at[i % 2]))
            copies[i].start()
    for copy in copies[-2:]:
        copy.wait()


def rest_products(hops, kept, where, tok, cot, both, third):
    width = third.shape[1]
    count = len(hops)
    vmem = pl.BlockSpec(memory_space=pltpu.VMEM)
    smem = pl.BlockSpec(memory_space=pltpu.SMEM)
    return pl.pallas_call(
        functools.partial(rest_kernel, hops),
        in_specs=[smem] + [vmem] * 4,
        out_specs=vmem if kept else pl.BlockSpec(memory_space=pltpu.HBM),
        scratch_shapes=[]
        if kept
        else [pltpu.VMEM((2, CHUNK, 3 * width), BF), pltpu.SemaphoreType.DMA((2,))],
        out_shape=(pltpu.VMEM if kept else pltpu.HBM)((count, CHUNK, 3 * width), BF),
        compiler_params=pltpu.CompilerParams(vmem_limit_bytes=12 * 2**20),
        cost_estimate=pl.CostEstimate(
            flops=12 * SEQ * CHUNK * count * width,
            bytes_accessed=count * CHUNK * (8 * SEQ + 6 * width),
            transcendentals=0,
        ),
    )(where, *map(in_vmem, (tok, cot, both, third)))


def backward_kernel(slots, gg_a, gu_a, gg_b, gu_b, gate, up, out, both):
    width = gate.shape[0]
    both[:SEQ, :] = jnp.concatenate([gg_a[...], gu_a[...]], 0).T
    both[SEQ:, :] = jnp.concatenate([gg_b[...], gu_b[...]], 0).T

    @pl.loop(0, D // TILE)
    def _(n):
        at = pl.ds(pl.multiple_of(n * TILE, TILE), TILE)
        value = jnp.dot(both[:, :width], gate[:, at], preferred_element_type=F32)
        value = value + jnp.dot(both[:, width:], up[:, at], preferred_element_type=F32)
        value = value.astype(BF).reshape(DEVICES, 16, TILE)
        for i in range(DEVICES):
            out[slots[i], :, at] = value[i]


def backward(slots, grads, gate_t, up_t):
    width = gate_t.shape[0]
    vmem = pl.BlockSpec(memory_space=pltpu.VMEM)
    return pl.pallas_call(
        backward_kernel,
        in_specs=[pl.BlockSpec(memory_space=pltpu.SMEM)] + [vmem] * 6,
        out_specs=vmem,
        scratch_shapes=[pltpu.VMEM((2 * SEQ, 2 * width), BF)],
        out_shape=pltpu.VMEM((DEVICES, 16, D), BF),
        compiler_params=pltpu.CompilerParams(vmem_limit_bytes=14 * 2**20),
        cost_estimate=pl.CostEstimate(
            flops=8 * SEQ * D * width,
            bytes_accessed=4 * D * width + 4 * SEQ * D + 8 * SEQ * width,
            transcendentals=0,
        ),
    )(slots, *map(in_vmem, (*grads, gate_t, up_t)))


def owners():
    table = np.zeros((DEVICES, DEVICES), np.int32)
    for place in range(DEVICES):
        x, y, core = place // (2 * NY), (place // 2) % NY, place % 2
        for at, example in enumerate((core, 1 - core)):
            for k in range(4):
                for j in range(NY):
                    near = (x - k) % NX
                    here = near // 2 == example
                    table[place, 16 * at + 4 * k + j] = flat(near if here else near + 2, y - j, 0 if here else 1)
    return table


def all_sum(value, beside):
    for perms in ([SWAP], [x_perm(k) for k in (1, 2, 3)], [y_perm(k) for k in (1, 2, 3)]):
        received = [send(value, p) for p in perms]
        if len(perms) > 1 and beside:
            received, beside = after(received, beside), None
        value = value + sum(received)
    return value


def exchange(value):
    return lax.all_to_all(value, "tensor", split_axis=0, concat_axis=0, tiled=True)


def body(tokens, cotangent, gate_weight, up_weight, down):
    place = lax.axis_index("tensor")
    where = jnp.stack([lax.axis_index("dp"), place % 2]).astype(jnp.int32)
    slots = lax.dynamic_index_in_dim(jnp.asarray(owners()), place, 0, False)
    order = jnp.where((jnp.arange(2) + place) % 2 == 0, 1.0, 0.0).astype(F32)[:, None]
    order = jnp.broadcast_to(order, (2, SEQ))
    tokens, cotangent, where, slots, order = lax.optimization_barrier(
        (tokens, cotangent, where, slots, order)
    )
    gate_t, up_t = gate_weight.T, up_weight.T
    tok_a, cot_a = gather(tokens, cotangent)
    tok_b = send(tok_a, SWAP)
    cot_b = send(cot_a, SWAP)
    hid_a, gg_a, gu_a, norm_a = example(tok_a, cot_a, gate_t, up_t, down)
    hid_b, gg_b, gu_b, norm_b = example(tok_b, cot_b, gate_t, up_t, down)
    pair = order * norm_a[None] + (1.0 - order) * norm_b[None]
    late, rows = lax.optimization_barrier(
        ((gg_a, gu_a, gg_b, gu_b), (tok_a, tok_b, cot_a, cot_b), pair)
    )[:2]
    turned_tok = turn(*rows[:2])
    turned_cot = turn(*rows[2:])
    norms = all_sum(pair, (turned_tok, turned_cot))
    grads = (gg_a, gu_a, hid_a, gg_b, gu_b, hid_b)
    firsts, both, third = first_products(where, norms, turned_tok, turned_cot, grads)
    seconds = second_products(where, turned_tok, turned_cot, both, third)

    rings = {s: [(i, (i + s) % NZ) for i in range(NZ)] for s in (1, -1)}
    held = firsts
    products = {}
    last = seconds
    for step in range(NZ - 1):
        if step == 0:
            local = dict(enumerate(seconds))
        else:
            local = {
                p: products[-s * (step + 2) % NZ][p * SUB : (p + 1) * SUB]
                for p, s in enumerate((1, 1, -1, -1))
            }
        for q in (0, 1):
            up = lax.ppermute(held[q], "dp", rings[1])
            down_ = lax.ppermute(held[q + 2], "dp", rings[-1])
            (up, down_), last = lax.optimization_barrier(((up, down_), last))
            last = [up.astype(F32) + local[q].astype(F32), down_.astype(F32) + local[q + 2].astype(F32)]
            if step < NZ - 2:
                last = [v.astype(BF) for v in last]
            held[q], held[q + 2] = last
        if step in (0, 2):
            hops = ((3, 5, 4), (6, 2, 7, 1, 0))[step // 2]
            later = after((turned_tok, turned_cot, both, third), last)
            fresh = rest_products(hops, step == 0, where, *later)
            products.update((hop, fresh[i]) for i, hop in enumerate(hops))
        if step == 1:
            partial = backward(slots, after(late, last), gate_t, up_t)
        if step == 3:
            returned = exchange(after(partial, last).reshape(DEVICES * 16, D))
        if step == 5:
            returned = after(returned, last)
            input_grad = jnp.sum(returned.reshape(DEVICES, 16, D).astype(F32), 0).astype(BF)
    totals = jnp.concatenate([held[p] for p in range(PARTS)], 0)
    width = gate_t.shape[0]
    return (
        input_grad,
        totals[:, :width],
        totals[:, width : 2 * width],
        totals[:, 2 * width :].T,
    )


def solution(mesh):
    rows = P(("dp", "tensor"), None)
    return jax.shard_map(
        body,
        mesh=mesh,
        in_specs=(rows, rows, P(None, "tensor"), P(None, "tensor"), P("tensor", None)),
        out_specs=(rows, P("dp", "tensor"), P("dp", "tensor"), P("tensor", "dp")),
        check_vma=False,
    )
```

```python
import functools
import math

import jax
import jax.numpy as jnp
import numpy as np
from jax import lax
from jax.experimental import pallas as pl
from jax.experimental.pallas import tpu as pltpu
from jax.sharding import PartitionSpec as P

D = 2304
FF = 18432
SEQ = 256
NX = 4
NY = 4
NZ = 8
CHUNK = D // NZ
PARTS = 4
HALF = CHUNK // 2
SUB = CHUNK // PARTS
DEVICES = 2 * NX * NY
TILE = 768
GELU_ROOT = math.sqrt(2.0 / math.pi)
GELU_CUBIC = 0.044715
BF = jnp.bfloat16
F32 = jnp.float32


def flat(x, y, c):
    return ((x % NX) * NY + (y % NY)) * 2 + c


def device_perm(move):
    return [
        (flat(x, y, c), flat(*move(x, y, c)))
        for x in range(NX)
        for y in range(NY)
        for c in range(2)
    ]


def y_perm(k):
    return device_perm(lambda x, y, c: (x, y + k, c))


def x_perm(k):
    return device_perm(lambda x, y, c: (x + k, y, c))


def round_perm(k):
    return device_perm(lambda x, y, c: (x + k + 2 * c, y, x // 2))


def inverse(perm):
    return [(b, a) for a, b in perm]


SWAP = device_perm(lambda x, y, c: (x, y, 1 - c))


def send(value, perm):
    return lax.ppermute(value, "tensor", perm)


def gelu_pair(value):
    inner = GELU_ROOT * (value + GELU_CUBIC * value * value * value)
    tangent = jnp.tanh(inner)
    activ = 0.5 * value * (1.0 + tangent)
    slope = 0.5 * (1.0 + tangent) + 0.5 * value * (1.0 - tangent * tangent) * GELU_ROOT * (
        1.0 + 3.0 * GELU_CUBIC * value * value
    )
    return (activ, slope)


def pack_kernel(tokens, cotangent, out, sems):
    copies = [
        pltpu.make_async_copy(tokens, out.at[:16], sems.at[0]),
        pltpu.make_async_copy(cotangent, out.at[16:], sems.at[1]),
    ]
    for copy in copies:
        copy.start()
    for copy in copies:
        copy.wait()


def pack(tokens, cotangent):
    hbm = pl.BlockSpec(memory_space=pltpu.HBM)
    return pl.pallas_call(
        pack_kernel,
        in_specs=[hbm, hbm],
        out_specs=pl.BlockSpec(memory_space=pltpu.VMEM),
        out_shape=pltpu.VMEM((32, D), BF),
        scratch_shapes=[pltpu.SemaphoreType.DMA((2,))],
        compiler_params=pltpu.CompilerParams(vmem_limit_bytes=2 * 2**20),
    )(*(pltpu.with_memory_space_constraint(v, pltpu.HBM) for v in (tokens, cotangent)))


def gather(tokens, cotangent, *scalars):
    shard = pack(tokens, cotangent)
    column = [shard] + [send(shard, y_perm(k)) for k in (1, 2, 3)]
    column, scalars = lax.optimization_barrier((column, scalars))
    column = jnp.concatenate([v[:16] for v in column] + [v[16:] for v in column], 0)
    rounds = [send(column, round_perm(k)) for k in range(4)]
    tok = jnp.concatenate([v[:64] for v in rounds], 0)
    return tok, jnp.concatenate([v[64:] for v in rounds], 0), *scalars


def after(value, *others):
    return lax.optimization_barrier((value, *others))[0]


def dot_nt(a, b):
    return lax.dot_general(a, b, (((1,), (1,)), ((), ())), preferred_element_type=F32)


def dot_tn(a, b):
    return lax.dot_general(a, b, (((0,), (0,)), ((), ())), preferred_element_type=F32)


def example(tok, cot, gate_t, up_t, down):
    pre_gate = dot_nt(gate_t, tok)
    pre_up = dot_nt(up_t, tok)
    activ, slope = gelu_pair(pre_gate)
    hidden = (activ * pre_up).astype(BF)
    grad_hidden = dot_nt(down, cot)
    grad_gate = (grad_hidden * pre_up * slope).astype(BF)
    grad_up = (grad_hidden * activ).astype(BF)
    norm = jnp.sum(
        dot_nt(tok, tok) * (dot_tn(grad_gate, grad_gate) + dot_tn(grad_up, grad_up))
        + dot_nt(cot, cot) * dot_tn(hidden, hidden),
        axis=0,
    )
    return hidden, grad_gate, grad_up, norm


def in_vmem(value):
    return pltpu.with_memory_space_constraint(value, pltpu.VMEM)


def turn_kernel(first, second, out):
    @pl.loop(0, D // 128)
    def _(i):
        at = pl.ds(pl.multiple_of(i * 128, 128), 128)
        out[at, :SEQ] = first[:, at].T
        out[at, SEQ:] = second[:, at].T


def turn(first, second):
    vmem = pl.BlockSpec(memory_space=pltpu.VMEM)
    return pl.pallas_call(
        turn_kernel,
        in_specs=[vmem, vmem],
        out_specs=vmem,
        out_shape=pltpu.VMEM((D, 2 * SEQ), BF),
        compiler_params=pltpu.CompilerParams(vmem_limit_bytes=12 * 2**20),
        cost_estimate=pl.CostEstimate(flops=4 * SEQ * D, bytes_accessed=8 * SEQ * D, transcendentals=0),
    )(in_vmem(first), in_vmem(second))


CLIP = math.sqrt(SEQ * D * (FF // 2 + D))
REACH = math.sqrt(D * FF)


def first_kernel(
    where, norms, tok, cot, gg_a, gu_a, hid_a, gg_b, gu_b, hid_b, up_0, up_1, down_0, down_1, both, third,
):
    factor = REACH / jnp.maximum(CLIP, jnp.sqrt(jnp.sum(norms[...], axis=1, keepdims=True)))
    mine = jnp.where(where[1] == 0, factor[:1], factor[1:])
    theirs = jnp.where(where[1] == 0, factor[1:], factor[:1])
    width = third.shape[1]
    for at, scale, (gg, gu, hid) in (
        (slice(0, SEQ), mine, (gg_a, gu_a, hid_a)),
        (slice(SEQ, 2 * SEQ), theirs, (gg_b, gu_b, hid_b)),
    ):
        joined = jnp.concatenate([gg[...], gu[...]], 0).astype(F32) * scale
        both[at, :] = joined.astype(BF).T
        third[at, :] = (hid[...].astype(F32) * scale).astype(BF).T

    fill_parts(where, tok, cot, both, third, (up_0, up_1, down_0, down_1), 1)


def fill_parts(where, tok, cot, both, third, parts, distance):
    width = third.shape[1]
    for hop, start, targets in ((NZ - distance, 0, parts[:2]), (distance, HALF, parts[2:])):
        chunk = lax.rem(where[0] + hop, NZ)
        at = pl.ds(pl.multiple_of(chunk * CHUNK + start, 16), HALF)
        left = jnp.dot(tok[at, :], both[...], preferred_element_type=F32)
        right = jnp.dot(cot[at, :], third[...], preferred_element_type=F32)
        for i, target in enumerate(targets):
            rows = slice(i * SUB, (i + 1) * SUB)
            target[:, : 2 * width] = left[rows].astype(BF)
            target[:, 2 * width :] = right[rows].astype(BF)


def first_products(where, norms, tok, cot, grads):
    width = grads[0].shape[0]
    vmem = pl.BlockSpec(memory_space=pltpu.VMEM)
    smem = pl.BlockSpec(memory_space=pltpu.SMEM)
    *firsts, both, third = pl.pallas_call(
        first_kernel,
        in_specs=[smem] + [vmem] * 9,
        out_specs=[vmem] * (PARTS + 2),
        out_shape=[pltpu.VMEM((SUB, 3 * width), BF)] * PARTS
        + [pltpu.VMEM((2 * SEQ, n * width), BF) for n in (2, 1)],
        compiler_params=pltpu.CompilerParams(vmem_limit_bytes=12 * 2**20),
        cost_estimate=pl.CostEstimate(
            flops=12 * SEQ * HALF * width, bytes_accessed=12 * SEQ * width, transcendentals=0
        ),
    )(where, *map(in_vmem, (norms, tok, cot, *grads)))
    return firsts, both, third


def second_kernel(where, tok, cot, both, third, up_0, up_1, down_0, down_1):
    fill_parts(where, tok, cot, both, third, (up_0, up_1, down_0, down_1), 2)


def second_products(where, tok, cot, both, third):
    width = third.shape[1]
    vmem = pl.BlockSpec(memory_space=pltpu.VMEM)
    smem = pl.BlockSpec(memory_space=pltpu.SMEM)
    return pl.pallas_call(
        second_kernel,
        in_specs=[smem] + [vmem] * 4,
        out_specs=[vmem] * PARTS,
        out_shape=[pltpu.VMEM((SUB, 3 * width), BF)] * PARTS,
        compiler_params=pltpu.CompilerParams(vmem_limit_bytes=8 * 2**20),
        cost_estimate=pl.CostEstimate(
            flops=12 * SEQ * HALF * width, bytes_accessed=12 * SEQ * width, transcendentals=0
        ),
    )(where, *map(in_vmem, (tok, cot, both, third)))


EARLY = ((3, 0, CHUNK), (5, 0, CHUNK), (4, 0, CHUNK))
LATE = ((2, 0, HALF), (6, HALF, HALF), (1, 0, HALF), (7, HALF, HALF), (0, 0, CHUNK))


def rest_kernel(items, where, tok, cot, both, third, out, *scratch):
    width = third.shape[1]
    copies, base = [], 0
    for i, (hop, start, rows) in enumerate(items):
        place = out.at[base : base + rows]
        base += rows
        target = place
        if scratch:
            ready, sems = scratch
            if i >= 2:
                copies[i - 2].wait()
            target = ready.at[i % 2, :rows]
        chunk = lax.rem(where[0] + hop, NZ)
        at = pl.ds(pl.multiple_of(chunk * CHUNK + start, 16), rows)
        target[:, : 2 * width] = jnp.dot(tok[at, :], both[...], preferred_element_type=F32).astype(BF)
        target[:, 2 * width :] = jnp.dot(cot[at, :], third[...], preferred_element_type=F32).astype(BF)
        if scratch:
            copies.append(pltpu.make_async_copy(target, place, sems.at[i % 2]))
            copies[i].start()
    for copy in copies[-2:]:
        copy.wait()


def rest_products(items, kept, where, tok, cot, both, third):
    width = third.shape[1]
    count = sum(rows for _, _, rows in items)
    vmem = pl.BlockSpec(memory_space=pltpu.VMEM)
    smem = pl.BlockSpec(memory_space=pltpu.SMEM)
    return pl.pallas_call(
        functools.partial(rest_kernel, items),
        in_specs=[smem] + [vmem] * 4,
        out_specs=vmem if kept else pl.BlockSpec(memory_space=pltpu.HBM),
        scratch_shapes=[]
        if kept
        else [pltpu.VMEM((2, CHUNK, 3 * width), BF), pltpu.SemaphoreType.DMA((2,))],
        out_shape=(pltpu.VMEM if kept else pltpu.HBM)((count, 3 * width), BF),
        compiler_params=pltpu.CompilerParams(vmem_limit_bytes=12 * 2**20),
        cost_estimate=pl.CostEstimate(
            flops=12 * SEQ * count * width,
            bytes_accessed=count * (8 * SEQ + 6 * width),
            transcendentals=0,
        ),
    )(where, *map(in_vmem, (tok, cot, both, third)))


def backward_kernel(slots, gg_a, gu_a, gg_b, gu_b, gate, up, out, both):
    width = gate.shape[0]
    both[:SEQ, :] = jnp.concatenate([gg_a[...], gu_a[...]], 0).T
    both[SEQ:, :] = jnp.concatenate([gg_b[...], gu_b[...]], 0).T

    @pl.loop(0, D // TILE)
    def _(n):
        at = pl.ds(pl.multiple_of(n * TILE, TILE), TILE)
        value = jnp.dot(both[:, :width], gate[:, at], preferred_element_type=F32)
        value = value + jnp.dot(both[:, width:], up[:, at], preferred_element_type=F32)
        value = value.astype(BF).reshape(DEVICES, 16, TILE)
        for i in range(DEVICES):
            out[slots[i], :, at] = value[i]


def backward(slots, grads, gate_t, up_t):
    width = gate_t.shape[0]
    vmem = pl.BlockSpec(memory_space=pltpu.VMEM)
    return pl.pallas_call(
        backward_kernel,
        in_specs=[pl.BlockSpec(memory_space=pltpu.SMEM)] + [vmem] * 6,
        out_specs=vmem,
        scratch_shapes=[pltpu.VMEM((2 * SEQ, 2 * width), BF)],
        out_shape=pltpu.VMEM((DEVICES, 16, D), BF),
        compiler_params=pltpu.CompilerParams(vmem_limit_bytes=14 * 2**20),
        cost_estimate=pl.CostEstimate(
            flops=8 * SEQ * D * width,
            bytes_accessed=4 * D * width + 4 * SEQ * D + 8 * SEQ * width,
            transcendentals=0,
        ),
    )(slots, *map(in_vmem, (*grads, gate_t, up_t)))


def owners():
    table = np.zeros((DEVICES, DEVICES), np.int32)
    for place in range(DEVICES):
        x, y, core = place // (2 * NY), (place // 2) % NY, place % 2
        for at, example in enumerate((core, 1 - core)):
            for k in range(4):
                for j in range(NY):
                    near = (x - k) % NX
                    here = near // 2 == example
                    table[place, 16 * at + 4 * k + j] = flat(near if here else near + 2, y - j, 0 if here else 1)
    return table


def all_sum(value, beside):
    for perms in ([SWAP], [x_perm(k) for k in (1, 2, 3)], [y_perm(k) for k in (1, 2, 3)]):
        received = [send(value, p) for p in perms]
        if len(perms) > 1 and beside:
            received, beside = after(received, beside), None
        value = value + sum(received)
    return value


def exchange(value):
    return lax.all_to_all(value, "tensor", split_axis=0, concat_axis=0, tiled=True)


def body(tokens, cotangent, gate_weight, up_weight, down):
    place = lax.axis_index("tensor")
    where = jnp.stack([lax.axis_index("dp"), place % 2]).astype(jnp.int32)
    slots = lax.dynamic_index_in_dim(jnp.asarray(owners()), place, 0, False)
    order = jnp.where((jnp.arange(2) + place) % 2 == 0, 1.0, 0.0).astype(F32)[:, None]
    order = jnp.broadcast_to(order, (2, SEQ))
    gate_t, up_t = gate_weight.T, up_weight.T
    tok_a, cot_a, where, slots, order = gather(tokens, cotangent, where, slots, order)
    tok_b = send(tok_a, SWAP)
    cot_b = send(cot_a, SWAP)
    hid_a, gg_a, gu_a, norm_a = example(tok_a, cot_a, gate_t, up_t, down)
    hid_b, gg_b, gu_b, norm_b = example(tok_b, cot_b, gate_t, up_t, down)
    pair = order * norm_a[None] + (1.0 - order) * norm_b[None]
    late, rows = lax.optimization_barrier(
        ((gg_a, gu_a, gg_b, gu_b), (tok_a, tok_b, cot_a, cot_b), pair)
    )[:2]
    turned_tok = turn(*rows[:2])
    turned_cot = turn(*rows[2:])
    norms = all_sum(pair, (turned_tok, turned_cot))
    grads = (gg_a, gu_a, hid_a, gg_b, gu_b, hid_b)
    firsts, both, third = first_products(where, norms, turned_tok, turned_cot, grads)
    seconds = second_products(where, turned_tok, turned_cot, both, third)

    rings = {s: [(i, (i + s) % NZ) for i in range(NZ)] for s in (1, -1)}
    held = firsts
    products = {}
    last = seconds
    for step in range(NZ - 1):
        if step == 0:
            local = dict(enumerate(seconds))
        else:
            local = {
                p: products[-s * (step + 2) % NZ, p]
                for p, s in enumerate((1, 1, -1, -1))
            }
        for q in (0, 1):
            up = lax.ppermute(held[q], "dp", rings[1])
            down_ = lax.ppermute(held[q + 2], "dp", rings[-1])
            (up, down_), last = lax.optimization_barrier(((up, down_), last))
            last = [up.astype(F32) + local[q].astype(F32), down_.astype(F32) + local[q + 2].astype(F32)]
            if step < NZ - 2:
                last = [v.astype(BF) for v in last]
            held[q], held[q + 2] = last
        if step in (0, 2):
            items = (EARLY, LATE)[step // 2]
            later = after((turned_tok, turned_cot, both, third), last)
            fresh = rest_products(items, step == 0, where, *later)
            base = 0
            for hop, start, rows in items:
                for p in range(start // SUB, (start + rows) // SUB):
                    products[hop, p] = fresh[base : base + SUB]
                    base += SUB
        if step == 1:
            partial = backward(slots, after(late, last), gate_t, up_t)
        if step == 3:
            returned = exchange(after(partial, last).reshape(DEVICES * 16, D))
        if step == 5:
            returned = after(returned, last)
            input_grad = jnp.sum(returned.reshape(DEVICES, 16, D).astype(F32), 0).astype(BF)
    totals = jnp.concatenate([held[p] for p in range(PARTS)], 0)
    width = gate_t.shape[0]
    return (
        input_grad,
        totals[:, :width],
        totals[:, width : 2 * width],
        totals[:, 2 * width :].T,
    )


def solution(mesh):
    rows = P(("dp", "tensor"), None)
    return jax.shard_map(
        body,
        mesh=mesh,
        in_specs=(rows, rows, P(None, "tensor"), P(None, "tensor"), P("tensor", None)),
        out_specs=(rows, P("dp", "tensor"), P("dp", "tensor"), P("tensor", "dp")),
        check_vma=False,
    )
```

```python
import functools
import math

import jax
import jax.numpy as jnp
import numpy as np
from jax import lax
from jax.experimental import pallas as pl
from jax.experimental.pallas import tpu as pltpu
from jax.sharding import PartitionSpec as P

D = 2304
FF = 18432
SEQ = 256
NX = 4
NY = 4
NZ = 8
CHUNK = D // NZ
PARTS = 4
HALF = CHUNK // 2
SUB = CHUNK // PARTS
DEVICES = 2 * NX * NY
TILE = 768
GELU_ROOT = math.sqrt(2.0 / math.pi)
GELU_CUBIC = 0.044715
BF = jnp.bfloat16
F32 = jnp.float32


def flat(x, y, c):
    return ((x % NX) * NY + (y % NY)) * 2 + c


def device_perm(move):
    return [
        (flat(x, y, c), flat(*move(x, y, c)))
        for x in range(NX)
        for y in range(NY)
        for c in range(2)
    ]


def y_perm(k):
    return device_perm(lambda x, y, c: (x, y + k, c))


def x_perm(k):
    return device_perm(lambda x, y, c: (x + k, y, c))


def round_perm(k):
    return device_perm(lambda x, y, c: (x + k + 2 * c, y, x // 2))


def inverse(perm):
    return [(b, a) for a, b in perm]


SWAP = device_perm(lambda x, y, c: (x, y, 1 - c))


def send(value, perm):
    return lax.ppermute(value, "tensor", perm)


def gelu_pair(value):
    inner = GELU_ROOT * (value + GELU_CUBIC * value * value * value)
    tangent = jnp.tanh(inner)
    activ = 0.5 * value * (1.0 + tangent)
    slope = 0.5 * (1.0 + tangent) + 0.5 * value * (1.0 - tangent * tangent) * GELU_ROOT * (
        1.0 + 3.0 * GELU_CUBIC * value * value
    )
    return (activ, slope)


def pack_kernel(tokens, cotangent, out, sems):
    copies = [
        pltpu.make_async_copy(tokens, out.at[:16], sems.at[0]),
        pltpu.make_async_copy(cotangent, out.at[16:], sems.at[1]),
    ]
    for copy in copies:
        copy.start()
    for copy in copies:
        copy.wait()


def pack(tokens, cotangent):
    hbm = pl.BlockSpec(memory_space=pltpu.HBM)
    return pl.pallas_call(
        pack_kernel,
        in_specs=[hbm, hbm],
        out_specs=pl.BlockSpec(memory_space=pltpu.VMEM),
        out_shape=pltpu.VMEM((32, D), BF),
        scratch_shapes=[pltpu.SemaphoreType.DMA((2,))],
        compiler_params=pltpu.CompilerParams(vmem_limit_bytes=2 * 2**20),
    )(*(pltpu.with_memory_space_constraint(v, pltpu.HBM) for v in (tokens, cotangent)))


def gather(tokens, cotangent, *scalars):
    shard = pack(tokens, cotangent)
    column = [shard] + [send(shard, y_perm(k)) for k in (1, 2, 3)]
    column, scalars = lax.optimization_barrier((column, scalars))
    column = jnp.concatenate([v[:16] for v in column] + [v[16:] for v in column], 0)
    rounds = [send(column, round_perm(k)) for k in range(4)]
    return jnp.concatenate([v[:64] for v in rounds] + [v[64:] for v in rounds], 0), *scalars


def after(value, *others):
    return lax.optimization_barrier((value, *others))[0]


def dot_nt(a, b):
    return lax.dot_general(a, b, (((1,), (1,)), ((), ())), preferred_element_type=F32)


def dot_tn(a, b):
    return lax.dot_general(a, b, (((0,), (0,)), ((), ())), preferred_element_type=F32)


def example(tok, cot, gate_t, up_t, down):
    pre_gate = dot_nt(gate_t, tok)
    pre_up = dot_nt(up_t, tok)
    activ, slope = gelu_pair(pre_gate)
    hidden = (activ * pre_up).astype(BF)
    grad_hidden = dot_nt(down, cot)
    grad_gate = (grad_hidden * pre_up * slope).astype(BF)
    grad_up = (grad_hidden * activ).astype(BF)
    norm = jnp.sum(
        dot_nt(tok, tok) * (dot_tn(grad_gate, grad_gate) + dot_tn(grad_up, grad_up))
        + dot_nt(cot, cot) * dot_tn(hidden, hidden),
        axis=0,
    )
    return hidden, grad_gate, grad_up, norm


def in_vmem(value):
    return pltpu.with_memory_space_constraint(value, pltpu.VMEM)


def turn_kernel(start, first, second, out):
    @pl.loop(0, D // 128)
    def _(i):
        at = pl.ds(pl.multiple_of(i * 128, 128), 128)
        out[at, :SEQ] = first[start : start + SEQ, at].T
        out[at, SEQ:] = second[start : start + SEQ, at].T


def turn(start, first, second):
    vmem = pl.BlockSpec(memory_space=pltpu.VMEM)
    return pl.pallas_call(
        functools.partial(turn_kernel, start),
        in_specs=[vmem, vmem],
        out_specs=vmem,
        out_shape=pltpu.VMEM((D, 2 * SEQ), BF),
        compiler_params=pltpu.CompilerParams(vmem_limit_bytes=12 * 2**20),
        cost_estimate=pl.CostEstimate(flops=4 * SEQ * D, bytes_accessed=8 * SEQ * D, transcendentals=0),
    )(in_vmem(first), in_vmem(second))


CLIP = math.sqrt(SEQ * D * (FF // 2 + D))
REACH = math.sqrt(D * FF)


def first_kernel(
    where, norms, tok, cot, gg_a, gu_a, hid_a, gg_b, gu_b, hid_b, up_0, up_1, down_0, down_1, both, third,
):
    factor = REACH / jnp.maximum(CLIP, jnp.sqrt(jnp.sum(norms[...], axis=1, keepdims=True)))
    mine = jnp.where(where[1] == 0, factor[:1], factor[1:])
    theirs = jnp.where(where[1] == 0, factor[1:], factor[:1])
    width = third.shape[1]
    for at, scale, (gg, gu, hid) in (
        (slice(0, SEQ), mine, (gg_a, gu_a, hid_a)),
        (slice(SEQ, 2 * SEQ), theirs, (gg_b, gu_b, hid_b)),
    ):
        joined = jnp.concatenate([gg[...], gu[...]], 0).astype(F32) * scale
        both[at, :] = joined.astype(BF).T
        third[at, :] = (hid[...].astype(F32) * scale).astype(BF).T

    fill_parts(where, tok, cot, both, third, (up_0, up_1, down_0, down_1), 1)


def fill_parts(where, tok, cot, both, third, parts, distance):
    width = third.shape[1]
    for hop, start, targets in ((NZ - distance, 0, parts[:2]), (distance, HALF, parts[2:])):
        chunk = lax.rem(where[0] + hop, NZ)
        at = pl.ds(pl.multiple_of(chunk * CHUNK + start, 16), HALF)
        left = jnp.dot(tok[at, :], both[...], preferred_element_type=F32)
        right = jnp.dot(cot[at, :], third[...], preferred_element_type=F32)
        for i, target in enumerate(targets):
            rows = slice(i * SUB, (i + 1) * SUB)
            target[:, : 2 * width] = left[rows].astype(BF)
            target[:, 2 * width :] = right[rows].astype(BF)


def first_products(where, norms, tok, cot, grads):
    width = grads[0].shape[0]
    vmem = pl.BlockSpec(memory_space=pltpu.VMEM)
    smem = pl.BlockSpec(memory_space=pltpu.SMEM)
    *firsts, both, third = pl.pallas_call(
        first_kernel,
        in_specs=[smem] + [vmem] * 9,
        out_specs=[vmem] * (PARTS + 2),
        out_shape=[pltpu.VMEM((SUB, 3 * width), BF)] * PARTS
        + [pltpu.VMEM((2 * SEQ, n * width), BF) for n in (2, 1)],
        compiler_params=pltpu.CompilerParams(vmem_limit_bytes=12 * 2**20),
        cost_estimate=pl.CostEstimate(
            flops=12 * SEQ * HALF * width, bytes_accessed=12 * SEQ * width, transcendentals=0
        ),
    )(where, *map(in_vmem, (norms, tok, cot, *grads)))
    return firsts, both, third


def second_kernel(where, tok, cot, both, third, up_0, up_1, down_0, down_1):
    fill_parts(where, tok, cot, both, third, (up_0, up_1, down_0, down_1), 2)


def second_products(where, tok, cot, both, third):
    width = third.shape[1]
    vmem = pl.BlockSpec(memory_space=pltpu.VMEM)
    smem = pl.BlockSpec(memory_space=pltpu.SMEM)
    return pl.pallas_call(
        second_kernel,
        in_specs=[smem] + [vmem] * 4,
        out_specs=[vmem] * PARTS,
        out_shape=[pltpu.VMEM((SUB, 3 * width), BF)] * PARTS,
        compiler_params=pltpu.CompilerParams(vmem_limit_bytes=8 * 2**20),
        cost_estimate=pl.CostEstimate(
            flops=12 * SEQ * HALF * width, bytes_accessed=12 * SEQ * width, transcendentals=0
        ),
    )(where, *map(in_vmem, (tok, cot, both, third)))


EARLY = ((3, 0, CHUNK), (5, 0, CHUNK), (4, 0, CHUNK))
LATE = ((2, 0, HALF), (6, HALF, HALF), (1, 0, HALF), (7, HALF, HALF), (0, 0, CHUNK))


def rest_kernel(items, where, tok, cot, both, third, out, *scratch):
    width = third.shape[1]
    copies, base = [], 0
    for i, (hop, start, rows) in enumerate(items):
        place = out.at[base : base + rows]
        base += rows
        target = place
        if scratch:
            ready, sems = scratch
            if i >= 2:
                copies[i - 2].wait()
            target = ready.at[i % 2, :rows]
        chunk = lax.rem(where[0] + hop, NZ)
        at = pl.ds(pl.multiple_of(chunk * CHUNK + start, 16), rows)
        target[:, : 2 * width] = jnp.dot(tok[at, :], both[...], preferred_element_type=F32).astype(BF)
        target[:, 2 * width :] = jnp.dot(cot[at, :], third[...], preferred_element_type=F32).astype(BF)
        if scratch:
            copies.append(pltpu.make_async_copy(target, place, sems.at[i % 2]))
            copies[i].start()
    for copy in copies[-2:]:
        copy.wait()


def rest_products(items, kept, where, tok, cot, both, third):
    width = third.shape[1]
    count = sum(rows for _, _, rows in items)
    vmem = pl.BlockSpec(memory_space=pltpu.VMEM)
    smem = pl.BlockSpec(memory_space=pltpu.SMEM)
    return pl.pallas_call(
        functools.partial(rest_kernel, items),
        in_specs=[smem] + [vmem] * 4,
        out_specs=vmem if kept else pl.BlockSpec(memory_space=pltpu.HBM),
        scratch_shapes=[]
        if kept
        else [pltpu.VMEM((2, CHUNK, 3 * width), BF), pltpu.SemaphoreType.DMA((2,))],
        out_shape=(pltpu.VMEM if kept else pltpu.HBM)((count, 3 * width), BF),
        compiler_params=pltpu.CompilerParams(vmem_limit_bytes=12 * 2**20),
        cost_estimate=pl.CostEstimate(
            flops=12 * SEQ * count * width,
            bytes_accessed=count * (8 * SEQ + 6 * width),
            transcendentals=0,
        ),
    )(where, *map(in_vmem, (tok, cot, both, third)))


def backward_kernel(slots, gg_a, gu_a, gg_b, gu_b, gate, up, out, both):
    width = gate.shape[0]
    both[:SEQ, :] = jnp.concatenate([gg_a[...], gu_a[...]], 0).T
    both[SEQ:, :] = jnp.concatenate([gg_b[...], gu_b[...]], 0).T

    @pl.loop(0, D // TILE)
    def _(n):
        at = pl.ds(pl.multiple_of(n * TILE, TILE), TILE)
        value = jnp.dot(both[:, :width], gate[:, at], preferred_element_type=F32)
        value = value + jnp.dot(both[:, width:], up[:, at], preferred_element_type=F32)
        value = value.astype(BF).reshape(DEVICES, 16, TILE)
        for i in range(DEVICES):
            out[slots[i], :, at] = value[i]


def backward(slots, grads, gate_t, up_t):
    width = gate_t.shape[0]
    vmem = pl.BlockSpec(memory_space=pltpu.VMEM)
    return pl.pallas_call(
        backward_kernel,
        in_specs=[pl.BlockSpec(memory_space=pltpu.SMEM)] + [vmem] * 6,
        out_specs=vmem,
        scratch_shapes=[pltpu.VMEM((2 * SEQ, 2 * width), BF)],
        out_shape=pltpu.VMEM((DEVICES, 16, D), BF),
        compiler_params=pltpu.CompilerParams(vmem_limit_bytes=14 * 2**20),
        cost_estimate=pl.CostEstimate(
            flops=8 * SEQ * D * width,
            bytes_accessed=4 * D * width + 4 * SEQ * D + 8 * SEQ * width,
            transcendentals=0,
        ),
    )(slots, *map(in_vmem, (*grads, gate_t, up_t)))


def owners():
    table = np.zeros((DEVICES, DEVICES), np.int32)
    for place in range(DEVICES):
        x, y, core = place // (2 * NY), (place // 2) % NY, place % 2
        for at, example in enumerate((core, 1 - core)):
            for k in range(4):
                for j in range(NY):
                    near = (x - k) % NX
                    here = near // 2 == example
                    table[place, 16 * at + 4 * k + j] = flat(near if here else near + 2, y - j, 0 if here else 1)
    return table


def all_sum(value, beside):
    for perms in ([SWAP], [x_perm(k) for k in (1, 2, 3)], [y_perm(k) for k in (1, 2, 3)]):
        received = [send(value, p) for p in perms]
        if len(perms) > 1 and beside:
            received, beside = after(received, beside), None
        value = value + sum(received)
    return value


def exchange(value):
    return lax.all_to_all(value, "tensor", split_axis=0, concat_axis=0, tiled=True)


def body(tokens, cotangent, gate_weight, up_weight, down):
    place = lax.axis_index("tensor")
    where = jnp.stack([lax.axis_index("dp"), place % 2]).astype(jnp.int32)
    slots = lax.dynamic_index_in_dim(jnp.asarray(owners()), place, 0, False)
    order = jnp.where((jnp.arange(2) + place) % 2 == 0, 1.0, 0.0).astype(F32)[:, None]
    order = jnp.broadcast_to(order, (2, SEQ))
    gate_t, up_t = gate_weight.T, up_weight.T
    rows_a, where, slots, order = gather(tokens, cotangent, where, slots, order)
    rows_b = send(rows_a, SWAP)
    tok_a, cot_a = rows_a[:SEQ], rows_a[SEQ:]
    tok_b, cot_b = rows_b[:SEQ], rows_b[SEQ:]
    hid_a, gg_a, gu_a, norm_a = example(tok_a, cot_a, gate_t, up_t, down)
    hid_b, gg_b, gu_b, norm_b = example(tok_b, cot_b, gate_t, up_t, down)
    pair = order * norm_a[None] + (1.0 - order) * norm_b[None]
    late, rows = lax.optimization_barrier(
        ((gg_a, gu_a, gg_b, gu_b), (rows_a, rows_b), pair)
    )[:2]
    turned_tok = turn(0, *rows)
    turned_cot = turn(SEQ, *rows)
    norms = all_sum(pair, (turned_tok, turned_cot))
    grads = (gg_a, gu_a, hid_a, gg_b, gu_b, hid_b)
    firsts, both, third = first_products(where, norms, turned_tok, turned_cot, grads)
    seconds = second_products(where, turned_tok, turned_cot, both, third)

    rings = {s: [(i, (i + s) % NZ) for i in range(NZ)] for s in (1, -1)}
    held = firsts
    products = {}
    last = seconds
    for step in range(NZ - 1):
        if step == 0:
            local = dict(enumerate(seconds))
        else:
            local = {
                p: products[-s * (step + 2) % NZ, p]
                for p, s in enumerate((1, 1, -1, -1))
            }
        for q in (0, 1):
            up = lax.ppermute(held[q], "dp", rings[1])
            down_ = lax.ppermute(held[q + 2], "dp", rings[-1])
            (up, down_), last = lax.optimization_barrier(((up, down_), last))
            last = [up.astype(F32) + local[q].astype(F32), down_.astype(F32) + local[q + 2].astype(F32)]
            if step < NZ - 2:
                last = [v.astype(BF) for v in last]
            held[q], held[q + 2] = last
        if step in (0, 2):
            items = (EARLY, LATE)[step // 2]
            later = after((turned_tok, turned_cot, both, third), last)
            fresh = rest_products(items, step == 0, where, *later)
            base = 0
            for hop, start, rows in items:
                for p in range(start // SUB, (start + rows) // SUB):
                    products[hop, p] = fresh[base : base + SUB]
                    base += SUB
        if step == 1:
            partial = backward(slots, after(late, last), gate_t, up_t)
        if step == 3:
            returned = exchange(after(partial, last).reshape(DEVICES * 16, D))
        if step == 5:
            returned = after(returned, last)
            input_grad = jnp.sum(returned.reshape(DEVICES, 16, D).astype(F32), 0).astype(BF)
    totals = jnp.concatenate([held[p] for p in range(PARTS)], 0)
    width = gate_t.shape[0]
    return (
        input_grad,
        totals[:, :width],
        totals[:, width : 2 * width],
        totals[:, 2 * width :].T,
    )


def solution(mesh):
    rows = P(("dp", "tensor"), None)
    return jax.shard_map(
        body,
        mesh=mesh,
        in_specs=(rows, rows, P(None, "tensor"), P(None, "tensor"), P("tensor", None)),
        out_specs=(rows, P("dp", "tensor"), P("dp", "tensor"), P("tensor", "dp")),
        check_vma=False,
    )
```

```python
import functools
import math

import jax
import jax.numpy as jnp
import numpy as np
from jax import lax
from jax.experimental import pallas as pl
from jax.experimental.pallas import tpu as pltpu
from jax.sharding import PartitionSpec as P

D = 2304
FF = 18432
SEQ = 256
NX = 4
NY = 4
NZ = 8
CHUNK = D // NZ
PARTS = 4
HALF = CHUNK // 2
SUB = CHUNK // PARTS
DEVICES = 2 * NX * NY
TILE = 1152
GELU_ROOT = math.sqrt(2.0 / math.pi)
GELU_CUBIC = 0.044715
BF = jnp.bfloat16
F32 = jnp.float32


def flat(x, y, c):
    return ((x % NX) * NY + (y % NY)) * 2 + c


def device_perm(move):
    return [
        (flat(x, y, c), flat(*move(x, y, c)))
        for x in range(NX)
        for y in range(NY)
        for c in range(2)
    ]


def y_perm(k):
    return device_perm(lambda x, y, c: (x, y + k, c))


def x_perm(k):
    return device_perm(lambda x, y, c: (x + k, y, c))


def round_perm(k):
    return device_perm(lambda x, y, c: (x + k + 2 * c, y, x // 2))


def inverse(perm):
    return [(b, a) for a, b in perm]


SWAP = device_perm(lambda x, y, c: (x, y, 1 - c))


def send(value, perm):
    return lax.ppermute(value, "tensor", perm)


def gelu_pair(value):
    inner = GELU_ROOT * (value + GELU_CUBIC * value * value * value)
    tangent = jnp.tanh(inner)
    activ = 0.5 * value * (1.0 + tangent)
    slope = 0.5 * (1.0 + tangent) + 0.5 * value * (1.0 - tangent * tangent) * GELU_ROOT * (
        1.0 + 3.0 * GELU_CUBIC * value * value
    )
    return (activ, slope)


def pack_kernel(tokens, cotangent, out, sems):
    copies = [
        pltpu.make_async_copy(tokens, out.at[:16], sems.at[0]),
        pltpu.make_async_copy(cotangent, out.at[16:], sems.at[1]),
    ]
    for copy in copies:
        copy.start()
    for copy in copies:
        copy.wait()


def pack(tokens, cotangent):
    hbm = pl.BlockSpec(memory_space=pltpu.HBM)
    return pl.pallas_call(
        pack_kernel,
        in_specs=[hbm, hbm],
        out_specs=pl.BlockSpec(memory_space=pltpu.VMEM),
        out_shape=pltpu.VMEM((32, D), BF),
        scratch_shapes=[pltpu.SemaphoreType.DMA((2,))],
        compiler_params=pltpu.CompilerParams(vmem_limit_bytes=2 * 2**20),
    )(*(pltpu.with_memory_space_constraint(v, pltpu.HBM) for v in (tokens, cotangent)))


def gather(tokens, cotangent, *scalars):
    shard = pack(tokens, cotangent)
    column = [shard] + [send(shard, y_perm(k)) for k in (1, 2, 3)]
    column, scalars = lax.optimization_barrier((column, scalars))
    column = jnp.concatenate([v[:16] for v in column] + [v[16:] for v in column], 0)
    rounds = [send(column, round_perm(k)) for k in range(4)]
    tok = jnp.concatenate([v[:64] for v in rounds], 0)
    return tok, jnp.concatenate([v[64:] for v in rounds], 0), *scalars


def after(value, *others):
    return lax.optimization_barrier((value, *others))[0]


def dot_nt(a, b):
    return lax.dot_general(a, b, (((1,), (1,)), ((), ())), preferred_element_type=F32)


def dot_tn(a, b):
    return lax.dot_general(a, b, (((0,), (0,)), ((), ())), preferred_element_type=F32)


def example(tok, cot, gate_t, up_t, down):
    pre_gate = dot_nt(gate_t, tok)
    pre_up = dot_nt(up_t, tok)
    activ, slope = gelu_pair(pre_gate)
    hidden = (activ * pre_up).astype(BF)
    grad_hidden = dot_nt(down, cot)
    grad_gate = (grad_hidden * pre_up * slope).astype(BF)
    grad_up = (grad_hidden * activ).astype(BF)
    norm = jnp.sum(
        dot_nt(tok, tok) * (dot_tn(grad_gate, grad_gate) + dot_tn(grad_up, grad_up))
        + dot_nt(cot, cot) * dot_tn(hidden, hidden),
        axis=0,
    )
    return hidden, grad_gate, grad_up, norm


def in_vmem(value):
    return pltpu.with_memory_space_constraint(value, pltpu.VMEM)


def turn_kernel(first, second, out):
    @pl.loop(0, D // 128)
    def _(i):
        at = pl.ds(pl.multiple_of(i * 128, 128), 128)
        out[at, :SEQ] = first[:, at].T
        out[at, SEQ:] = second[:, at].T


def turn(first, second):
    vmem = pl.BlockSpec(memory_space=pltpu.VMEM)
    return pl.pallas_call(
        turn_kernel,
        in_specs=[vmem, vmem],
        out_specs=vmem,
        out_shape=pltpu.VMEM((D, 2 * SEQ), BF),
        compiler_params=pltpu.CompilerParams(vmem_limit_bytes=12 * 2**20),
        cost_estimate=pl.CostEstimate(flops=4 * SEQ * D, bytes_accessed=8 * SEQ * D, transcendentals=0),
    )(in_vmem(first), in_vmem(second))


CLIP = math.sqrt(SEQ * D * (FF // 2 + D))
REACH = math.sqrt(D * FF)


def first_kernel(
    where, norms, tok, cot, gg_a, gu_a, hid_a, gg_b, gu_b, hid_b, up_0, up_1, down_0, down_1, both, third,
):
    factor = REACH / jnp.maximum(CLIP, jnp.sqrt(jnp.sum(norms[...], axis=1, keepdims=True)))
    mine = jnp.where(where[1] == 0, factor[:1], factor[1:])
    theirs = jnp.where(where[1] == 0, factor[1:], factor[:1])
    width = third.shape[1]
    for at, scale, (gg, gu, hid) in (
        (slice(0, SEQ), mine, (gg_a, gu_a, hid_a)),
        (slice(SEQ, 2 * SEQ), theirs, (gg_b, gu_b, hid_b)),
    ):
        joined = jnp.concatenate([gg[...], gu[...]], 0).astype(F32) * scale
        both[at, :] = joined.astype(BF).T
        third[at, :] = (hid[...].astype(F32) * scale).astype(BF).T

    fill_parts(where, tok, cot, both, third, (up_0, up_1, down_0, down_1), 1)


def fill_parts(where, tok, cot, both, third, parts, distance):
    width = third.shape[1]
    for hop, start, targets in ((NZ - distance, 0, parts[:2]), (distance, HALF, parts[2:])):
        chunk = lax.rem(where[0] + hop, NZ)
        at = pl.ds(pl.multiple_of(chunk * CHUNK + start, 16), HALF)
        left = jnp.dot(tok[at, :], both[...], preferred_element_type=F32)
        right = jnp.dot(cot[at, :], third[...], preferred_element_type=F32)
        for i, target in enumerate(targets):
            rows = slice(i * SUB, (i + 1) * SUB)
            target[:, : 2 * width] = left[rows].astype(BF)
            target[:, 2 * width :] = right[rows].astype(BF)


def first_products(where, norms, tok, cot, grads):
    width = grads[0].shape[0]
    vmem = pl.BlockSpec(memory_space=pltpu.VMEM)
    smem = pl.BlockSpec(memory_space=pltpu.SMEM)
    *firsts, both, third = pl.pallas_call(
        first_kernel,
        in_specs=[smem] + [vmem] * 9,
        out_specs=[vmem] * (PARTS + 2),
        out_shape=[pltpu.VMEM((SUB, 3 * width), BF)] * PARTS
        + [pltpu.VMEM((2 * SEQ, n * width), BF) for n in (2, 1)],
        compiler_params=pltpu.CompilerParams(vmem_limit_bytes=12 * 2**20),
        cost_estimate=pl.CostEstimate(
            flops=12 * SEQ * HALF * width, bytes_accessed=12 * SEQ * width, transcendentals=0
        ),
    )(where, *map(in_vmem, (norms, tok, cot, *grads)))
    return firsts, both, third


def second_kernel(where, tok, cot, both, third, up_0, up_1, down_0, down_1):
    fill_parts(where, tok, cot, both, third, (up_0, up_1, down_0, down_1), 2)


def second_products(where, tok, cot, both, third):
    width = third.shape[1]
    vmem = pl.BlockSpec(memory_space=pltpu.VMEM)
    smem = pl.BlockSpec(memory_space=pltpu.SMEM)
    return pl.pallas_call(
        second_kernel,
        in_specs=[smem] + [vmem] * 4,
        out_specs=[vmem] * PARTS,
        out_shape=[pltpu.VMEM((SUB, 3 * width), BF)] * PARTS,
        compiler_params=pltpu.CompilerParams(vmem_limit_bytes=8 * 2**20),
        cost_estimate=pl.CostEstimate(
            flops=12 * SEQ * HALF * width, bytes_accessed=12 * SEQ * width, transcendentals=0
        ),
    )(where, *map(in_vmem, (tok, cot, both, third)))


EARLY = ((3, 0, CHUNK), (5, 0, CHUNK), (4, 0, CHUNK))
LATE = ((2, 0, HALF), (6, HALF, HALF), (1, 0, HALF), (7, HALF, HALF), (0, 0, CHUNK))


def rest_kernel(items, where, tok, cot, both, third, out, *scratch):
    width = third.shape[1]
    copies, base = [], 0
    for i, (hop, start, rows) in enumerate(items):
        place = out.at[base : base + rows]
        base += rows
        target = place
        if scratch:
            ready, sems = scratch
            if i >= 2:
                copies[i - 2].wait()
            target = ready.at[i % 2, :rows]
        chunk = lax.rem(where[0] + hop, NZ)
        at = pl.ds(pl.multiple_of(chunk * CHUNK + start, 16), rows)
        target[:, : 2 * width] = jnp.dot(tok[at, :], both[...], preferred_element_type=F32).astype(BF)
        target[:, 2 * width :] = jnp.dot(cot[at, :], third[...], preferred_element_type=F32).astype(BF)
        if scratch:
            copies.append(pltpu.make_async_copy(target, place, sems.at[i % 2]))
            copies[i].start()
    for copy in copies[-2:]:
        copy.wait()


def rest_products(items, kept, where, tok, cot, both, third):
    width = third.shape[1]
    count = sum(rows for _, _, rows in items)
    vmem = pl.BlockSpec(memory_space=pltpu.VMEM)
    smem = pl.BlockSpec(memory_space=pltpu.SMEM)
    return pl.pallas_call(
        functools.partial(rest_kernel, items),
        in_specs=[smem] + [vmem] * 4,
        out_specs=vmem if kept else pl.BlockSpec(memory_space=pltpu.HBM),
        scratch_shapes=[]
        if kept
        else [pltpu.VMEM((2, CHUNK, 3 * width), BF), pltpu.SemaphoreType.DMA((2,))],
        out_shape=(pltpu.VMEM if kept else pltpu.HBM)((count, 3 * width), BF),
        compiler_params=pltpu.CompilerParams(vmem_limit_bytes=12 * 2**20),
        cost_estimate=pl.CostEstimate(
            flops=12 * SEQ * count * width,
            bytes_accessed=count * (8 * SEQ + 6 * width),
            transcendentals=0,
        ),
    )(where, *map(in_vmem, (tok, cot, both, third)))


def backward_kernel(slots, gg_a, gu_a, gg_b, gu_b, gate, up, out, both):
    width = gate.shape[0]
    both[:SEQ, :] = jnp.concatenate([gg_a[...], gu_a[...]], 0).T
    both[SEQ:, :] = jnp.concatenate([gg_b[...], gu_b[...]], 0).T

    @pl.loop(0, D // TILE)
    def _(n):
        at = pl.ds(pl.multiple_of(n * TILE, TILE), TILE)
        value = jnp.dot(both[:, :width], gate[:, at], preferred_element_type=F32)
        value = value + jnp.dot(both[:, width:], up[:, at], preferred_element_type=F32)
        value = value.astype(BF).reshape(DEVICES, 16, TILE)
        for i in range(DEVICES):
            out[slots[i], :, at] = value[i]


def backward(slots, grads, gate_t, up_t):
    width = gate_t.shape[0]
    vmem = pl.BlockSpec(memory_space=pltpu.VMEM)
    return pl.pallas_call(
        backward_kernel,
        in_specs=[pl.BlockSpec(memory_space=pltpu.SMEM)] + [vmem] * 6,
        out_specs=vmem,
        scratch_shapes=[pltpu.VMEM((2 * SEQ, 2 * width), BF)],
        out_shape=pltpu.VMEM((DEVICES, 16, D), BF),
        compiler_params=pltpu.CompilerParams(vmem_limit_bytes=14 * 2**20),
        cost_estimate=pl.CostEstimate(
            flops=8 * SEQ * D * width,
            bytes_accessed=4 * D * width + 4 * SEQ * D + 8 * SEQ * width,
            transcendentals=0,
        ),
    )(slots, *map(in_vmem, (*grads, gate_t, up_t)))


def owners():
    table = np.zeros((DEVICES, DEVICES), np.int32)
    for place in range(DEVICES):
        x, y, core = place // (2 * NY), (place // 2) % NY, place % 2
        for at, example in enumerate((core, 1 - core)):
            for k in range(4):
                for j in range(NY):
                    near = (x - k) % NX
                    here = near // 2 == example
                    table[place, 16 * at + 4 * k + j] = flat(near if here else near + 2, y - j, 0 if here else 1)
    return table


def all_sum(value, beside):
    for perms in ([SWAP], [x_perm(k) for k in (1, 2, 3)], [y_perm(k) for k in (1, 2, 3)]):
        received = [send(value, p) for p in perms]
        if len(perms) > 1 and beside:
            received, beside = after(received, beside), None
        value = value + sum(received)
    return value


def exchange(value):
    return lax.all_to_all(value, "tensor", split_axis=0, concat_axis=0, tiled=True)


def body(tokens, cotangent, gate_weight, up_weight, down):
    place = lax.axis_index("tensor")
    where = jnp.stack([lax.axis_index("dp"), place % 2]).astype(jnp.int32)
    slots = lax.dynamic_index_in_dim(jnp.asarray(owners()), place, 0, False)
    order = jnp.where((jnp.arange(2) + place) % 2 == 0, 1.0, 0.0).astype(F32)[:, None]
    order = jnp.broadcast_to(order, (2, SEQ))
    gate_t, up_t = gate_weight.T, up_weight.T
    tok_a, cot_a, where, slots, order = gather(tokens, cotangent, where, slots, order)
    tok_b = send(tok_a, SWAP)
    cot_b = send(cot_a, SWAP)
    hid_a, gg_a, gu_a, norm_a = example(tok_a, cot_a, gate_t, up_t, down)
    hid_b, gg_b, gu_b, norm_b = example(tok_b, cot_b, gate_t, up_t, down)
    pair = order * norm_a[None] + (1.0 - order) * norm_b[None]
    late, rows = lax.optimization_barrier(
        ((gg_a, gu_a, gg_b, gu_b), (tok_a, tok_b, cot_a, cot_b), pair)
    )[:2]
    turned_tok = turn(*rows[:2])
    turned_cot = turn(*rows[2:])
    norms = all_sum(pair, (turned_tok, turned_cot))
    grads = (gg_a, gu_a, hid_a, gg_b, gu_b, hid_b)
    firsts, both, third = first_products(where, norms, turned_tok, turned_cot, grads)
    seconds = second_products(where, turned_tok, turned_cot, both, third)

    rings = {s: [(i, (i + s) % NZ) for i in range(NZ)] for s in (1, -1)}
    held = firsts
    products = {}
    last = seconds
    for step in range(NZ - 1):
        if step == 0:
            local = dict(enumerate(seconds))
        else:
            local = {
                p: products[-s * (step + 2) % NZ, p]
                for p, s in enumerate((1, 1, -1, -1))
            }
        for q in (0, 1):
            up = lax.ppermute(held[q], "dp", rings[1])
            down_ = lax.ppermute(held[q + 2], "dp", rings[-1])
            (up, down_), last = lax.optimization_barrier(((up, down_), last))
            last = [up.astype(F32) + local[q].astype(F32), down_.astype(F32) + local[q + 2].astype(F32)]
            if step < NZ - 2:
                last = [v.astype(BF) for v in last]
            held[q], held[q + 2] = last
        if step in (0, 2):
            items = (EARLY, LATE)[step // 2]
            later = after((turned_tok, turned_cot, both, third), last)
            fresh = rest_products(items, step == 0, where, *later)
            base = 0
            for hop, start, rows in items:
                for p in range(start // SUB, (start + rows) // SUB):
                    products[hop, p] = fresh[base : base + SUB]
                    base += SUB
        if step == 1:
            partial = backward(slots, after(late, last), gate_t, up_t)
        if step == 3:
            returned = exchange(after(partial, last).reshape(DEVICES * 16, D))
        if step == 5:
            returned = after(returned, last)
            input_grad = jnp.sum(returned.reshape(DEVICES, 16, D).astype(F32), 0).astype(BF)
    totals = jnp.concatenate([held[p] for p in range(PARTS)], 0)
    width = gate_t.shape[0]
    return (
        input_grad,
        totals[:, :width],
        totals[:, width : 2 * width],
        totals[:, 2 * width :].T,
    )


def solution(mesh):
    rows = P(("dp", "tensor"), None)
    return jax.shard_map(
        body,
        mesh=mesh,
        in_specs=(rows, rows, P(None, "tensor"), P(None, "tensor"), P("tensor", None)),
        out_specs=(rows, P("dp", "tensor"), P("dp", "tensor"), P("tensor", "dp")),
        check_vma=False,
    )
```
